32 devices in a mesh: dp: 8 (over y, x, core), tensor: 4 (over z).
Axes of the slice: x: 2, y: 2, z: 4, core: 2. Of those that a mesh axis runs over, the one named last changes fastest.
Arguments:
- tokens: bfloat16 [8192, 2048], P(('dp', 'tensor')), may hold values from -6 to 6
- attn_gain: bfloat16 [2048], replicated, may hold values from 0.099609375 to 1.8984375
- query_gain: bfloat16 [2048], P('tensor'), may hold values from 0.099609375 to 1.8984375
- key_gain: bfloat16 [2048], P('tensor'), may hold values from 0.099609375 to 1.8984375
- query_weight: bfloat16 [2048, 2048], P('dp', 'tensor'), may hold values from -0.125 to 0.125
- key_weight: bfloat16 [2048, 2048], P('dp', 'tensor'), may hold values from -0.125 to 0.125
- value_weight: bfloat16 [2048, 2048], P('dp', 'tensor'), may hold values from -0.125 to 0.125
- output_weight: bfloat16 [2048, 2048], P('tensor', 'dp'), may hold values from -2 to 2
- mlp_gain: bfloat16 [2048], replicated, may hold values from 0.099609375 to 1.8984375
- router_weight: bfloat16 [2048, 16], P('dp'), may hold values from -0.046875 to 0.046875
- gate_weight: bfloat16 [16, 2048, 1024], P(None, 'dp', 'tensor'), may hold values from -0.125 to 0.125
- up_weight: bfloat16 [16, 2048, 1024], P(None, 'dp', 'tensor'), may hold values from -0.125 to 0.125
- down_weight: bfloat16 [16, 1024, 2048], P(None, 'tensor', 'dp'), may hold values from -1.5 to 1.5
- query_lower: bfloat16 [8, 2048, 16], replicated, may hold values from -0.125 to 0.125
- query_raise: bfloat16 [8, 16, 2048], P(None, None, 'tensor'), may hold values from -0.75 to 0.75
- key_lower: bfloat16 [8, 2048, 16], replicated, may hold values from -0.125 to 0.125
- key_raise: bfloat16 [8, 16, 2048], P(None, None, 'tensor'), may hold values from -0.75 to 0.75
- value_lower: bfloat16 [8, 2048, 16], replicated, may hold values from -0.125 to 0.125
- value_raise: bfloat16 [8, 16, 2048], P(None, None, 'tensor'), may hold values from -0.75 to 0.75
- output_lower: bfloat16 [8, 2048, 16], P(None, 'tensor'), may hold values from -2 to 2
- output_raise: bfloat16 [8, 16, 2048], replicated, may hold values from -0.75 to 0.75
- routes: int32 [8192, 8], P('dp'), may hold values from 0 to 15, all different within a row; in each aligned block of 1024 rows (0 to 1023, 1024 to 2047, ...) at most 768 rows name the same one
- adapter_choice_rows: int32 [8], P('dp'), may hold values from 0 to 7
- out_cotangent: bfloat16 [8192, 2048], P(('dp', 'tensor')), may hold values from -6 to 6
Outputs:
- block_out: bfloat16 [8192, 2048], P(('dp', 'tensor'))
- input_grad: bfloat16 [8192, 2048], P(('dp', 'tensor'))
- grad_query_lower: float32 [8, 2048, 16], replicated
- grad_query_raise: float32 [8, 16, 2048], P(None, None, 'tensor')
- grad_key_lower: float32 [8, 2048, 16], replicated
- grad_key_raise: float32 [8, 16, 2048], P(None, None, 'tensor')
- grad_value_lower: float32 [8, 2048, 16], replicated
- grad_value_raise: float32 [8, 16, 2048], P(None, None, 'tensor')
- grad_output_lower: float32 [8, 2048, 16], P(None, 'tensor')
- grad_output_raise: float32 [8, 16, 2048], replicated
The draws below stay inside these ranges and needn't reach their ends.
Inputs may be any that keep to these rules, and one draw needn't show every extreme that they name: `routes`: each row names 8 different experts. In each aligned block of 1024 rows (the tokens of one index of dp) no expert is named by more than 768 rows, and in some block one expert is named by exactly 768 rows.
All inputs are finite; a program needn't handle non-finite values.
Results may differ from the reference program's by a relative error of at most 0.02.
Values may be sent and summed in bfloat16 or wider, within the bound.
No kernel may reach another device: no remote copies, remote signals or barrier semaphores. Data moves between devices by JAX's collectives and lax.ppermute only.
A program may use at most 256 MiB of HBM per device.

```python
import math
import jax
import jax.numpy as jnp
import numpy as np
from jax import lax

D = 2048
HEADS = 16
HEAD_DIM = 128
FF = 1024
TOP = 8
EXPERTS = 16
RANK = 16
ADAPTERS = 8
SEQUENCE_TOKENS = 1024
SEQUENCES_PER_DATA = 1
GROUP_TOK = 1024
ROUTE_MOST = 768
SEQS = 8
TOKENS = 8192
N_DP = 8


def touch_ends(values, own_key, low, high):
    shape = values.shape
    index_at = [jax.random.randint(jax.random.fold_in(own_key, axis), (), 0, shape[axis]) for axis in range(len(shape))]
    values = values.at[tuple(index_at)].set(low)
    longest = shape.index(max(shape))
    index_at[longest] = (index_at[longest] + 1) % shape[longest]
    return values.at[tuple(index_at)].set(high)


def levels(rng, shape, pieces, low, high):
    loudness = 1.0
    for axis_at, blocks in pieces:
        draws = jax.random.uniform(jax.random.fold_in(jax.random.fold_in(rng, 6), axis_at), (blocks,), jnp.float32, low / len(pieces), high / len(pieces))
        loudness = loudness * jnp.repeat(jnp.exp(draws), shape[axis_at] // blocks).reshape((-1,) + (1,) * (len(shape) - 1 - axis_at))
    return loudness


def routed_block(key, own, number, rows, number_of, top, reach, lean):
    order = jax.random.permutation(key, number_of)
    heavy_load, usual = shares(number_of, rows * top, reach, lean, True), shares(number_of, rows * top, reach, lean, False)
    places = jnp.arange(number_of)

    def named(tallies, turn):
        used = int((tallies > 0).sum())
        fixed = max(1, used // 4)
        passed = fixed + (places - fixed + turn * (used - fixed)) % max(1, number_of - fixed)
        return jnp.zeros((number_of,), jnp.int32).at[order[jnp.where(places < fixed, places, passed)]].set(jnp.asarray(tallies, jnp.int32))

    tallies = jnp.where(number % 4 == 0, named(heavy_load, number // 4), named(usual, number - number // 4 - 1))
    mixed = jax.random.permutation(jax.random.fold_in(own, 3), number_of)
    donor, receiver = mixed[0:number_of // 2 * 2:2], mixed[1:number_of // 2 * 2:2]
    room = jnp.minimum(tallies[donor] - 1, reach - tallies[receiver]) // 2
    room = jnp.where((donor == order[0]) | (receiver == order[0]) | (tallies[receiver] == 0), 0, jnp.maximum(room, 0))
    passed = jax.random.randint(jax.random.fold_in(own, 4), (number_of // 2,), 0, 1 << 20) % (room + 1)
    tallies = tallies.at[donor].add(-passed).at[receiver].add(passed)
    labels = jnp.searchsorted(jnp.cumsum(tallies), jnp.arange(rows * top), side="right").astype(jnp.int32)
    listing = labels.reshape(top, rows).T
    listing = listing[jax.random.permutation(jax.random.fold_in(own, 1), rows)]
    turn = jax.random.randint(jax.random.fold_in(own, 2), (rows, 1), 0, top)
    return jnp.take_along_axis(listing, (jnp.arange(top)[None, :] + turn) % top, axis=1)


def shares(number_of, total, limit, slope, full):
    portions = [(1 << 20) // math.isqrt(grade ** slope) + 1 for grade in range(1, number_of + 1)]
    largest = limit if full else min(limit, max(-(-total // number_of), total * portions[0] // sum(portions)))
    least = 1 if total - largest >= number_of - 1 else 0
    given, surplus = [largest] + [least] * (number_of - 1), total - largest - least * (number_of - 1)
    while surplus > 0:
        candidates = [i for i in range(1, number_of) if given[i] < largest] or [i for i in range(1, number_of) if given[i] < limit]
        pool, left = sum([portions[i] for i in candidates]), surplus
        for i in candidates:
            more = min(limit - given[i], max(1, left * portions[i] // pool), surplus)
            given[i] = given[i] + more
            surplus = surplus - more
    return np.array(given)


def noise(rng, extent, scale, reach, shards=(), held_as=jnp.bfloat16):
    drawn = scale * jax.random.normal(rng, extent, jnp.float32)
    if shards:
        drawn = drawn * levels(rng, extent, shards, -0.22, 0.18)
    return jnp.clip(drawn, -reach, reach).astype(held_as)


def setup_inputs(seed: int = 0) -> dict:
    splits = jax.random.split(jax.random.key(seed), 25)
    tokens = noise(splits[0], (TOKENS, D), 1.0, 6.0, ((0, 32),))
    attn_gain = jnp.clip(1.0 + 0.18 * jax.random.normal(splits[1], (D,), jnp.float32), 0.099609375, 1.8984375).astype(jnp.bfloat16)
    query_gain = jnp.clip(1.0 + 0.18 * jax.random.normal(splits[2], (D,), jnp.float32), 0.099609375, 1.8984375).astype(jnp.bfloat16)
    key_gain = jnp.clip(1.0 + 0.18 * jax.random.normal(splits[3], (D,), jnp.float32), 0.099609375, 1.8984375).astype(jnp.bfloat16)
    query_weight = noise(splits[4], (D, D), D ** -0.5, 0.125, ((0, 8), (1, 4)))
    key_weight = noise(splits[5], (D, D), D ** -0.5, 0.125, ((0, 8), (1, 4)))
    value_weight = noise(splits[6], (D, D), D ** -0.5, 0.125, ((0, 8), (1, 4)))
    output_weight = noise(splits[7], (D, D), (max(4 * D // SEQUENCE_TOKENS, 1)) ** -0.5, 2.0, ((0, 4), (1, 8)))
    mlp_gain = jnp.clip(1.0 + 0.18 * jax.random.normal(splits[8], (D,), jnp.float32), 0.099609375, 1.8984375).astype(jnp.bfloat16)
    router_weight = noise(splits[9], (D, EXPERTS), (8 * D) ** -0.5, 0.046875, ((0, 8),))
    gate_weight = noise(splits[10], (EXPERTS, D, FF), D ** -0.5, 0.125, ((1, 8), (2, 4)))
    up_weight = noise(splits[11], (EXPERTS, D, FF), D ** -0.5, 0.125, ((1, 8), (2, 4)))
    down_weight = noise(splits[12], (EXPERTS, FF, D), (max(FF // 64, 1)) ** -0.5, 1.5, ((1, 4), (2, 8)))
    query_lower = noise(splits[13], (ADAPTERS, D, RANK), D ** -0.5, 0.125)
    query_raise = noise(splits[14], (ADAPTERS, RANK, D), (4 * RANK) ** -0.5, 0.75, ((2, 4),))
    key_lower = noise(splits[15], (ADAPTERS, D, RANK), D ** -0.5, 0.125)
    key_raise = noise(splits[16], (ADAPTERS, RANK, D), (4 * RANK) ** -0.5, 0.75, ((2, 4),))
    value_lower = noise(splits[17], (ADAPTERS, D, RANK), D ** -0.5, 0.125)
    value_raise = noise(splits[18], (ADAPTERS, RANK, D), (4 * RANK) ** -0.5, 0.75, ((2, 4),))
    output_lower = noise(splits[19], (ADAPTERS, D, RANK), (max(4 * D // SEQUENCE_TOKENS, 1)) ** -0.5, 2.0, ((1, 4),))
    output_raise = noise(splits[20], (ADAPTERS, RANK, D), (4 * RANK) ** -0.5, 0.75)
    routes_keys = jax.random.split(jax.random.fold_in(splits[21], 1), TOKENS // GROUP_TOK)
    routes_turns = jax.random.permutation(jax.random.fold_in(splits[21], 3), TOKENS // GROUP_TOK)
    routes = jax.vmap(lambda own, number: routed_block(jax.random.fold_in(splits[21], 2), own, number, GROUP_TOK, EXPERTS, TOP, ROUTE_MOST, 2))(routes_keys, routes_turns).reshape((TOKENS, TOP))
    adapter_choice_rows = touch_ends(jax.random.randint(splits[22], (SEQS,), 0, ADAPTERS), jax.random.fold_in(splits[22], 1), 0, ADAPTERS - 1).astype(jnp.int32)
    out_cotangent = noise(splits[23], (TOKENS, D), 1.0, 6.0, ((0, 32),))
    return {"tokens": tokens, "attn_gain": attn_gain, "query_gain": query_gain, "key_gain": key_gain, "query_weight": query_weight, "key_weight": key_weight, "value_weight": value_weight, "output_weight": output_weight, "mlp_gain": mlp_gain, "router_weight": router_weight, "gate_weight": gate_weight, "up_weight": up_weight, "down_weight": down_weight, "query_lower": query_lower, "query_raise": query_raise, "key_lower": key_lower, "key_raise": key_raise, "value_lower": value_lower, "value_raise": value_raise, "output_lower": output_lower, "output_raise": output_raise, "routes": routes, "adapter_choice_rows": adapter_choice_rows, "out_cotangent": out_cotangent}


EPSILON = 1e-05
ROPE_BASE = 10000.0
PRECISION_BEST = lax.Precision.HIGHEST
MASKED = -1e+30

@jax.custom_vjp
def low(v):
    return lax.optimization_barrier(v.astype(jnp.bfloat16)).astype(jnp.float32)

@jax.custom_vjp
def low_back(v):
    return v

def low_keep(v):
    return (low(v), None)

def low_pass(kept, grad):
    return (grad,)

def back_keep(v):
    return (v, None)

def back_low(kept, grad):
    return (low(grad),)
low.defvjp(low_keep, low_pass)
low_back.defvjp(back_keep, back_low)

def product(left, right):
    return jnp.dot(left, right, precision=PRECISION_BEST, preferred_element_type=jnp.float32)

def to_float(values):
    return values.astype(jnp.float32)

def norm_rows(values, gain_row):
    inverse = lax.rsqrt(lax.optimization_barrier(jnp.mean(values * values, axis=-1, keepdims=True)) + EPSILON)
    return values * inverse * gain_row

def rope_tables(row_count):
    position = (jnp.arange(row_count, dtype=jnp.int32) % SEQUENCE_TOKENS).astype(jnp.float32)
    frequency = ROPE_BASE ** (-2.0 * jnp.arange(HEAD_DIM // 2, dtype=jnp.float32) / HEAD_DIM)
    angles = position[:, None] * frequency[None, :]
    return (jnp.cos(angles), jnp.sin(angles))

def rotate(head_rows, cosine_table, sine_table):
    half_dim = HEAD_DIM // 2
    former = head_rows[..., :half_dim]
    latter = head_rows[..., half_dim:]
    cos_wide = cosine_table[:, None, :]
    sin_wide = sine_table[:, None, :]
    return jnp.concatenate([former * cos_wide - latter * sin_wide, latter * cos_wide + former * sin_wide], axis=-1)

def slot_table(routes):
    expert_row = jnp.arange(EXPERTS, dtype=jnp.int32)
    chosen = lax.optimization_barrier(jnp.sum((routes[:, :, None] == expert_row[None, None, :]).astype(jnp.int32), axis=1)).astype(jnp.int32)
    placed = (jnp.cumsum(chosen, axis=0) - 1).astype(jnp.int32)
    target = jnp.where(chosen == 1, placed, ROUTE_MOST).astype(jnp.int32)
    token_row = jnp.broadcast_to(jnp.arange(routes.shape[0], dtype=jnp.int32)[:, None], chosen.shape)
    expert_col = jnp.broadcast_to(expert_row[None, :], chosen.shape)
    slot_rows = jnp.zeros((EXPERTS, ROUTE_MOST + 1), jnp.int32).at[expert_col, target].set(token_row)
    slot_live = jnp.zeros((EXPERTS, ROUTE_MOST + 1), jnp.float32).at[expert_col, target].set(1.0)
    return (slot_rows[:, :ROUTE_MOST], slot_live[:, :ROUTE_MOST])

def attention(queries, key_rows, value_rows):
    block_rows = min(512, SEQUENCE_TOKENS)
    blocks = SEQUENCE_TOKENS // block_rows
    scale_factor = HEAD_DIM ** (-0.5)
    seq_queries = queries.reshape(SEQUENCES_PER_DATA, SEQUENCE_TOKENS, HEADS, HEAD_DIM)
    seq_keys = key_rows.reshape(SEQUENCES_PER_DATA, SEQUENCE_TOKENS, HEADS, HEAD_DIM)
    seq_values = value_rows.reshape(SEQUENCES_PER_DATA, SEQUENCE_TOKENS, HEADS, HEAD_DIM)

    def one_block(position):
        sequence = position // blocks
        portion = position % blocks
        these_queries = lax.dynamic_slice_in_dim(lax.dynamic_index_in_dim(seq_queries, sequence, 0, keepdims=False), portion * block_rows, block_rows, 0)
        these_keys = lax.dynamic_index_in_dim(seq_keys, sequence, 0, keepdims=False)
        these_values = lax.dynamic_index_in_dim(seq_values, sequence, 0, keepdims=False)
        scores = jnp.einsum('qhd,khd->hqk', these_queries, these_keys, precision=PRECISION_BEST) * scale_factor
        scores = low_back(scores)
        query_pos = portion * block_rows + jnp.arange(block_rows, dtype=jnp.int32)
        allowed = jnp.arange(SEQUENCE_TOKENS, dtype=jnp.int32)[None, :] <= query_pos[:, None]
        scores = jnp.where(allowed[None, :, :], scores, MASKED)
        soft_rows = jax.nn.softmax(scores, axis=-1)
        return jnp.einsum('hqk,khd->qhd', low(soft_rows), these_values, precision=PRECISION_BEST)
    result = lax.map(jax.checkpoint(one_block), jnp.arange(SEQUENCES_PER_DATA * blocks, dtype=jnp.int32))
    return result.reshape(GROUP_TOK, HEADS * HEAD_DIM)

def group_forward(rows_in, adapters, frozen, routes, adapter_choice_rows, cosine_table, sine_table):
    attn_gain, query_gain, key_gain, query_weight, key_weight, value_weight, output_weight, mlp_gain, router_weight, gate_weight, up_weight, down_weight = frozen
    query_lower, query_raise, key_lower, key_raise, value_lower, value_raise, output_lower, output_raise = adapters
    normed = low(norm_rows(rows_in, attn_gain))

    def project(inputs, weight, downward_product, upward):
        base_part = product(inputs, weight)
        sequence_adapter = inputs.reshape(SEQUENCES_PER_DATA, SEQUENCE_TOKENS, inputs.shape[-1])
        middle_product = jnp.einsum('zmp,zpo->zmo', sequence_adapter, downward_product[adapter_choice_rows], precision=PRECISION_BEST)
        side_part = jnp.einsum('slr,sre->sle', middle_product, upward[adapter_choice_rows], precision=PRECISION_BEST)
        return base_part + side_part.reshape(GROUP_TOK, weight.shape[1])
    query_raw = low_back(project(normed, query_weight, query_lower, query_raise))
    key_raw = low_back(project(normed, key_weight, key_lower, key_raise))
    value_raw = low_back(project(normed, value_weight, value_lower, value_raise))

    def prepare(raw_rows, gain_row):
        heads_view = norm_rows(raw_rows, gain_row).reshape(GROUP_TOK, HEADS, HEAD_DIM)
        return low(rotate(heads_view, cosine_table, sine_table))
    queries = prepare(query_raw, query_gain)
    key_rows = prepare(key_raw, key_gain)
    value_rows = low(value_raw).reshape(GROUP_TOK, HEADS, HEAD_DIM)
    attention_result = low_back(low(attention(queries, key_rows, value_rows)))
    attn_out = low_back(project(attention_result, output_weight, output_lower, output_raise))
    hidden_one = rows_in + attn_out
    normed_two = low(norm_rows(hidden_one, mlp_gain))
    logits = low_back(product(normed_two, router_weight))
    route_prob = jax.nn.softmax(logits, axis=-1)
    slot_rows, slot_live = slot_table(routes)
    slot_weight = route_prob[slot_rows, jnp.arange(EXPERTS, dtype=jnp.int32)[:, None]] * slot_live

    def expert_step(running, item_set):
        expert_gate, expert_up, expert_down, row_index, slot_scale = item_set
        picked = normed_two[row_index]
        gate_val = low_back(product(picked, expert_gate))
        up_val = low_back(product(picked, expert_up))
        activated = low(jax.nn.silu(gate_val) * up_val)
        expert_out = low_back(product(activated, expert_down))
        return (running.at[row_index].add(slot_scale[:, None] * expert_out), None)
    moe_sum, _ = lax.scan(jax.checkpoint(expert_step), jnp.zeros((GROUP_TOK, D), jnp.float32), (gate_weight, up_weight, down_weight, slot_rows, slot_weight))
    return hidden_one + moe_sum

def reference(tokens, attn_gain, query_gain, key_gain, query_weight, key_weight, value_weight, output_weight, mlp_gain, router_weight, gate_weight, up_weight, down_weight, query_lower, query_raise, key_lower, key_raise, value_lower, value_raise, output_lower, output_raise, routes, adapter_choice_rows, out_cotangent):
    frozen = tuple((to_float(item_set) for item_set in (attn_gain, query_gain, key_gain, query_weight, key_weight, value_weight, output_weight, mlp_gain, router_weight, gate_weight, up_weight, down_weight)))
    adapters = tuple((to_float(item_set) for item_set in (query_lower, query_raise, key_lower, key_raise, value_lower, value_raise, output_lower, output_raise)))
    cosine_table, sine_table = rope_tables(GROUP_TOK)
    token_groups = to_float(tokens).reshape(N_DP, GROUP_TOK, D)
    grad_groups = to_float(out_cotangent).reshape(N_DP, GROUP_TOK, D)
    route_groups = routes.reshape(N_DP, GROUP_TOK, TOP)
    pick_groups = adapter_choice_rows.reshape(N_DP, SEQUENCES_PER_DATA)

    def group_step(totals, item_set):
        rows_in, rows_grad, group_routes, group_pick = item_set

        def forward(values_in, adapter_set):
            return group_forward(values_in, adapter_set, frozen, group_routes, group_pick, cosine_table, sine_table)
        result, pullback = jax.vjp(forward, rows_in, adapters)
        grad_rows, grad_adapters = pullback(rows_grad)
        totals = jax.tree.map(lambda left, right: left + right, totals, grad_adapters)
        return (totals, (result.astype(jnp.bfloat16), grad_rows.astype(jnp.bfloat16)))
    zero_grads = jax.tree.map(jnp.zeros_like, adapters)
    totals, (out_rows, grad_rows) = lax.scan(group_step, zero_grads, (token_groups, grad_groups, route_groups, pick_groups))
    return (out_rows.reshape(TOKENS, D), grad_rows.reshape(TOKENS, D), totals[0], totals[1], totals[2], totals[3], totals[4], totals[5], totals[6], totals[7])
```

```python
import functools

import jax
import jax.numpy as jnp
from jax import lax
from jax.experimental import pallas as pl
from jax.experimental.pallas import tpu as pltpu
from jax.sharding import PartitionSpec as P

HEAD_DIM = 128
EPSILON = 1e-05
ROPE_BASE = 10000.0
MASKED = -1e30
MIB = 1024 * 1024

f32 = jnp.float32
bf16 = jnp.bfloat16


def nn(left, right):
    return jnp.dot(left, right, preferred_element_type=f32)


def nt(left, right):
    return lax.dot_general(left, right, (((1,), (1,)), ((), ())), preferred_element_type=f32)


def tn(left, right):
    return lax.dot_general(left, right, (((0,), (0,)), ((), ())), preferred_element_type=f32)


def after(value, *others):
    return lax.optimization_barrier((value,) + others)[0]


def line_gather(unit, axis, count):
    me = lax.axis_index(axis)
    rows = unit.shape[0]
    rights, lefts = [unit], [unit]
    for step in range(1, count):
        rights.append(
            lax.ppermute(rights[-1], axis, [(i, i + 1) for i in range(step - 1, count - 1)])
        )
        lefts.append(
            lax.ppermute(lefts[-1], axis, [(i, i - 1) for i in range(1, count - step + 1)])
        )
    whole = jnp.zeros((count * rows,) + unit.shape[1:], unit.dtype)
    whole = lax.dynamic_update_slice_in_dim(whole, unit, me * rows, 0)
    for step in range(1, count):
        piece = jnp.where(me >= step, rights[step], lefts[count - step])
        place = lax.rem(me - step + count, count)
        whole = lax.dynamic_update_slice_in_dim(whole, piece, place * rows, 0)
    return whole


def line_scatter(parts, axis, count):
    me = lax.axis_index(axis)
    rows = parts.shape[0] // count

    def own(index):
        return lax.dynamic_slice_in_dim(parts, index * rows, rows, 0).astype(f32)

    right = left = None
    for step in range(1, count):
        to_right = own(jnp.clip(count - step + me, 0, count - 1))
        to_left = own(jnp.clip(me + step - count, 0, count - 1))
        if right is not None:
            to_right = to_right + right.astype(f32)
            to_left = to_left + left.astype(f32)
        right = lax.ppermute(
            to_right.astype(bf16), axis, [(i, i + 1) for i in range(min(step, count - 1))]
        )
        left = lax.ppermute(
            to_left.astype(bf16),
            axis,
            [(i, i - 1) for i in range(count - 1, max(count - 1 - step, 0), -1)],
        )
    return own(me) + right.astype(f32) + left.astype(f32)


def direct_scatter(parts, axis, count):
    me = lax.axis_index(axis)
    rows = parts.shape[0] // count
    total = lax.dynamic_slice_in_dim(parts, me * rows, rows, 0).astype(f32)
    for shift in range(1, count):
        target = lax.rem(me + shift, count)
        part = lax.dynamic_slice_in_dim(parts, target * rows, rows, 0)
        got = lax.ppermute(part, axis, [(i, (i + shift) % count) for i in range(count)])
        total = total + got.astype(f32)
    return total


def direct_sum(value, axis, count):
    total = value
    for shift in range(1, count):
        total = total + lax.ppermute(
            value, axis, [(i, (i + shift) % count) for i in range(count)]
        )
    return total


def rope_tables(row_count):
    position = jnp.arange(row_count, dtype=jnp.int32).astype(f32)
    half = HEAD_DIM // 2
    frequency = ROPE_BASE ** (-2.0 * jnp.arange(half, dtype=f32) / HEAD_DIM)
    angles = position[:, None] * frequency[None, :]
    cosine, sine = jnp.cos(angles), jnp.sin(angles)
    return (
        jnp.concatenate([cosine, cosine], axis=1),
        jnp.concatenate([-sine, sine], axis=1),
    )


def causal_scores(q_block, keys, first):
    scores = nt(q_block, keys) * (HEAD_DIM**-0.5)
    rows = first + lax.broadcasted_iota(jnp.int32, scores.shape, 0)
    columns = lax.broadcasted_iota(jnp.int32, scores.shape, 1)
    return jnp.where(columns <= rows, scores, MASKED)


def attend_kernel(
    block,
    query_raw,
    key_raw,
    value_raw,
    query_inverse,
    key_inverse,
    query_gain,
    key_gain,
    cosine,
    sine,
    queries,
    keys,
    values,
    attended,
    log_sums,
):
    half = HEAD_DIM // 2
    rows = query_raw.shape[0]

    def rotated(raw, inverse, gain):
        head = raw[...] * inverse[...] * gain[...]
        return (head * cosine[...] + pltpu.roll(head, half, 1) * sine[...]).astype(bf16)

    queries[...] = rotated(query_raw, query_inverse, query_gain)
    keys[...] = rotated(key_raw, key_inverse, key_gain)
    values[...] = value_raw[...].astype(bf16)
    for first in range(0, rows, block):
        end = first + block
        here = slice(first, end)
        scores = causal_scores(queries[here, :], keys[0:end, :], first)
        top = jnp.max(scores, axis=1, keepdims=True)
        exponent = jnp.exp(scores - top)
        total = jnp.sum(exponent, axis=1, keepdims=True)
        soft = (exponent * (1.0 / total)).astype(bf16)
        attended[here, :] = nn(soft, values[0:end, :]).astype(bf16)
        log_sums[0, here, :] = top + jnp.log(total)


def attend(raws, inverses, gains, tables):
    rows, width = raws[0].shape
    heads = width // HEAD_DIM
    by_head = pl.BlockSpec((rows, HEAD_DIM), lambda h: (0, h))
    column = pl.BlockSpec((rows, 1), lambda h: (0, 0))
    gain = pl.BlockSpec((1, HEAD_DIM), lambda h: (0, h))
    table = pl.BlockSpec((rows, HEAD_DIM), lambda h: (0, 0))
    wide = jax.ShapeDtypeStruct((rows, width), bf16)
    return pl.pallas_call(
        functools.partial(attend_kernel, min(256, rows)),
        grid=(heads,),
        in_specs=[by_head] * 3 + [column] * 2 + [gain] * 2 + [table] * 2,
        out_specs=[by_head] * 4 + [pl.BlockSpec((1, rows, 1), lambda h: (h, 0, 0))],
        out_shape=[wide] * 4 + [jax.ShapeDtypeStruct((heads, rows, 1), f32)],
        compiler_params=pltpu.CompilerParams(vmem_limit_bytes=40 * MIB),
        cost_estimate=pl.CostEstimate(
            flops=2 * rows * rows * width,
            bytes_accessed=20 * rows * width,
            transcendentals=rows * rows * heads // 2,
        ),
    )(*raws, *inverses, *gains, *tables)


def attend_back_kernel(
    block,
    queries,
    keys,
    values,
    grads,
    log_sums,
    query_raw,
    key_raw,
    query_inverse,
    key_inverse,
    query_gain,
    key_gain,
    cosine,
    sine,
    query_out,
    key_out,
    value_out,
    query_dot,
    key_dot,
    query_grad,
    key_grad,
    value_grad,
):
    half = HEAD_DIM // 2
    rows = queries.shape[0]
    scale = HEAD_DIM**-0.5
    for first in range(rows - block, -1, -block):
        end = first + block
        here = slice(first, end)
        scores = causal_scores(queries[here, :], keys[0:end, :], first)
        soft = jnp.exp(scores - log_sums[0, here, :])
        soft_grad = nt(grads[here, :], values[0:end, :])
        inner = jnp.sum(soft * soft_grad, axis=1, keepdims=True)
        score_grad = (soft * (soft_grad - inner)).astype(bf16)
        value_part = tn(soft.astype(bf16), grads[here, :])
        key_part = tn(score_grad, queries[here, :])
        query_grad[here, :] = nn(score_grad, keys[0:end, :])
        if end == rows:
            value_grad[...] = value_part
            key_grad[...] = key_part
        else:
            value_grad[0:end, :] += value_part
            key_grad[0:end, :] += key_part

    def pulled(grad, raw, inverse, gain, out, dot):
        turned = grad[...] * scale
        turned = turned * cosine[...] - pltpu.roll(turned, half, 1) * sine[...]
        turned = turned * gain[...]
        out[...] = turned
        partial = jnp.sum(turned * (raw[...] * inverse[...]), axis=1, keepdims=True)

        @pl.when(pl.program_id(0) == 0)
        def _():
            dot[...] = partial

        @pl.when(pl.program_id(0) > 0)
        def _():
            dot[...] += partial

    pulled(query_grad, query_raw, query_inverse, query_gain, query_out, query_dot)
    pulled(key_grad, key_raw, key_inverse, key_gain, key_out, key_dot)
    value_out[...] = value_grad[...].astype(bf16)


def attend_back(heads_in, grads, log_sums, raws, inverses, gains, tables):
    rows, width = grads.shape
    heads = width // HEAD_DIM
    by_head = pl.BlockSpec((rows, HEAD_DIM), lambda h: (0, h))
    column = pl.BlockSpec((rows, 1), lambda h: (0, 0))
    gain = pl.BlockSpec((1, HEAD_DIM), lambda h: (0, h))
    table = pl.BlockSpec((rows, HEAD_DIM), lambda h: (0, 0))
    return pl.pallas_call(
        functools.partial(attend_back_kernel, min(256, rows)),
        grid=(heads,),
        in_specs=[by_head] * 4
        + [pl.BlockSpec((1, rows, 1), lambda h: (h, 0, 0))]
        + [by_head] * 2
        + [column] * 2
        + [gain] * 2
        + [table] * 2,
        out_specs=[by_head] * 3 + [column] * 2,
        out_shape=[
            jax.ShapeDtypeStruct((rows, width), f32),
            jax.ShapeDtypeStruct((rows, width), f32),
            jax.ShapeDtypeStruct((rows, width), bf16),
            jax.ShapeDtypeStruct((rows, 1), f32),
            jax.ShapeDtypeStruct((rows, 1), f32),
        ],
        scratch_shapes=[pltpu.VMEM((rows, HEAD_DIM), f32)] * 3,
        compiler_params=pltpu.CompilerParams(vmem_limit_bytes=40 * MIB),
        cost_estimate=pl.CostEstimate(
            flops=5 * rows * rows * width,
            bytes_accessed=28 * rows * width,
            transcendentals=rows * rows * heads // 2,
        ),
    )(*heads_in, grads, log_sums, *raws[:2], *inverses, *gains, *tables)


def experts_kernel(
    rows_in, grads, weight, gates, ups, downs, moe, back, slots, moe_sum, back_sum
):
    expert = pl.program_id(0)
    pieces, _, hidden, wide = downs.shape
    depth = pieces * wide
    gate_matrix = gates[:, 0].reshape(depth, hidden)
    up_matrix = ups[:, 0].reshape(depth, hidden)
    gate = nn(rows_in[...], gate_matrix)
    up = nn(rows_in[...], up_matrix)
    inner = nt(grads[:, 0:wide], downs[0, 0])
    for piece in range(1, pieces):
        inner += nt(grads[:, piece * wide : (piece + 1) * wide], downs[piece, 0])
    lane = lax.broadcasted_iota(jnp.int32, weight.shape, 1)
    row_scale = jnp.sum(jnp.where(lane == expert, weight[...], 0.0), axis=1, keepdims=True)
    sigmoid = jax.nn.sigmoid(gate)
    silu = gate * sigmoid
    activated = (silu * up).astype(bf16).astype(f32)
    slot = jnp.sum(activated * inner, axis=1, keepdims=True)
    scaled = (row_scale * activated).astype(bf16)
    inner = row_scale * inner
    gate_grad = (inner * up * (sigmoid * (1.0 + gate * (1.0 - sigmoid)))).astype(bf16)
    up_grad = (inner * silu).astype(bf16)

    @pl.when(expert == 0)
    def _():
        slots[...] = jnp.where(lane == expert, slot, 0.0)
        for piece in range(pieces):
            moe_sum[:, piece * wide : (piece + 1) * wide] = nn(scaled, downs[piece, 0])
        back_sum[...] = nt(gate_grad, gate_matrix) + nt(up_grad, up_matrix)

    @pl.when(expert > 0)
    def _():
        slots[...] = jnp.where(lane == expert, slot, slots[...])
        for piece in range(pieces):
            moe_sum[:, piece * wide : (piece + 1) * wide] += nn(scaled, downs[piece, 0])
        back_sum[...] += nt(gate_grad, gate_matrix) + nt(up_grad, up_matrix)

    @pl.when(expert == pl.num_programs(0) - 1)
    def _():
        moe[...] = moe_sum[...].astype(bf16)
        back[...] = back_sum[...].astype(bf16)


def experts_both(rows_in, grads, weight, gates, ups, downs):
    rows, depth = rows_in.shape
    pieces, experts, hidden, wide = downs.shape

    def fixed(shape):
        return pl.BlockSpec(shape, lambda e: (0, 0), pipeline_mode=pl.Buffered(1))

    def of_expert(shape):
        return pl.BlockSpec((shape[0], 1) + shape[2:], lambda e: (0, e, 0, 0))

    return pl.pallas_call(
        experts_kernel,
        grid=(experts,),
        in_specs=[
            fixed((rows, depth)),
            fixed((rows, depth)),
            fixed((rows, experts)),
            of_expert(gates.shape),
            of_expert(ups.shape),
            of_expert(downs.shape),
        ],
        out_specs=[fixed((rows, depth)), fixed((rows, depth)), fixed((rows, experts))],
        out_shape=[
            jax.ShapeDtypeStruct((rows, depth), bf16),
            jax.ShapeDtypeStruct((rows, depth), bf16),
            jax.ShapeDtypeStruct((rows, experts), f32),
        ],
        scratch_shapes=[pltpu.VMEM((rows, depth), f32), pltpu.VMEM((rows, depth), f32)],
        compiler_params=pltpu.CompilerParams(vmem_limit_bytes=60 * MIB),
        cost_estimate=pl.CostEstimate(
            flops=12 * rows * depth * hidden * experts,
            bytes_accessed=6 * depth * hidden * experts,
            transcendentals=rows * hidden * experts,
        ),
    )(rows_in, grads, weight, gates, ups, downs)


def norm_back(values, gain, grad):
    inverse = lax.rsqrt(jnp.mean(values * values, axis=-1, keepdims=True) + EPSILON)
    scaled = values * inverse
    inner = gain * grad
    return inverse * (inner - scaled * jnp.mean(inner * scaled, axis=-1, keepdims=True))


def norm_rows(values, gain):
    inverse = lax.rsqrt(jnp.mean(values * values, axis=-1, keepdims=True) + EPSILON)
    return values * inverse * gain


def per_device(
    n_data,
    n_tensor,
    tokens,
    attn_gain,
    query_gain,
    key_gain,
    query_weight,
    key_weight,
    value_weight,
    output_weight,
    mlp_gain,
    router_weight,
    gate_weight,
    up_weight,
    down_weight,
    query_lower,
    query_raise,
    key_lower,
    key_raise,
    value_lower,
    value_raise,
    output_lower,
    output_raise,
    routes,
    adapter_choice_rows,
    out_cotangent,
):
    local_rows, depth = tokens.shape
    rows = local_rows * n_tensor
    width = query_weight.shape[1]
    adapters, rank = query_raise.shape[:2]
    experts = router_weight.shape[1]
    me = lax.axis_index("tensor")
    first_row = me * local_rows
    adapter = adapter_choice_rows[0]

    def chosen(table):
        return lax.dynamic_index_in_dim(table, adapter, 0, keepdims=False)

    def columns_of(matrix):
        return lax.dynamic_slice_in_dim(matrix, me * width, width, 1)

    tables = rope_tables(rows)
    attn_gain_wide = attn_gain.astype(f32)
    mlp_gain_wide = mlp_gain.astype(f32)
    gains = (query_gain.astype(f32)[None, :], key_gain.astype(f32)[None, :])
    expert_ids = jnp.arange(experts, dtype=jnp.int32)
    route_mask = jnp.any(routes[:, :, None] == expert_ids[None, None, :], axis=1).astype(f32)

    projections = lax.all_gather(
        jnp.concatenate([query_weight, key_weight, value_weight], axis=1),
        "dp",
        axis=0,
        tiled=True,
    )
    output_and_router = lax.all_gather(
        jnp.concatenate([output_weight, router_weight.T], axis=0), "dp", axis=0
    )
    output_full = output_and_router[:, :width].transpose(1, 0, 2).reshape(width, depth)
    router_full = output_and_router[:, width:].transpose(1, 0, 2).reshape(experts, depth)
    gates = lax.all_gather(gate_weight, "dp", axis=0)
    ups = lax.all_gather(up_weight, "dp", axis=0)
    downs = lax.all_gather(down_weight, "dp", axis=0)

    rows_float = tokens.astype(f32)
    normed_local = norm_rows(rows_float, attn_gain_wide).astype(bf16)
    normed = line_gather(normed_local, "tensor", n_tensor)
    cotangent_full = line_gather(after(out_cotangent, normed), "tensor", n_tensor)

    lowers = jnp.concatenate(
        [chosen(query_lower).T, chosen(key_lower).T, chosen(value_lower).T], axis=0
    )
    raises = [chosen(query_raise), chosen(key_raise), chosen(value_raise)]
    mids = nt(normed, lowers).astype(bf16)
    raws = [
        nn(normed, projections[:, i * width : (i + 1) * width])
        + nn(mids[:, i * rank : (i + 1) * rank], raises[i])
        for i in range(3)
    ]
    totals = jnp.stack([jnp.sum(raws[0] * raws[0], axis=1), jnp.sum(raws[1] * raws[1], axis=1)])
    totals = direct_sum(totals, "tensor", n_tensor)
    inverse_rows = lax.rsqrt(totals / depth + EPSILON)
    inverses = (inverse_rows[0][:, None], inverse_rows[1][:, None])
    queries, keys, values, attended, log_sums = attend(raws, inverses, gains, tables)

    output_down = chosen(output_lower).T
    output_up = chosen(output_raise)
    output_mid = nt(attended, output_down)
    attn_part = nn(attended, output_full) + nn(output_mid.astype(bf16), output_up)
    hidden_one = rows_float + line_scatter(attn_part.astype(bf16), "tensor", n_tensor)

    normed_two = line_gather(
        norm_rows(hidden_one, mlp_gain_wide).astype(bf16), "tensor", n_tensor
    )
    route_prob = jax.nn.softmax(nt(normed_two, router_full), axis=-1)
    moe_part, back_part, slot_part = experts_both(
        normed_two, cotangent_full, route_prob * route_mask, gates, ups, downs
    )
    back_local = lax.psum_scatter(back_part, "tensor", scatter_dimension=0, tiled=True)
    prob_grad = direct_scatter((slot_part * route_mask).astype(bf16), "tensor", n_tensor)
    prob_local = lax.dynamic_slice_in_dim(route_prob, first_row, local_rows, 0)
    logit_grad = (
        prob_local * (prob_grad - jnp.sum(prob_local * prob_grad, axis=1, keepdims=True))
    ).astype(bf16)
    normed_two_grad = back_local.astype(f32) + nn(logit_grad, router_full)
    hidden_grad = out_cotangent.astype(f32) + norm_back(
        hidden_one, mlp_gain_wide, normed_two_grad
    )
    attn_grad = lax.all_gather(hidden_grad.astype(bf16), "tensor", axis=0, tiled=True)
    moe_local = lax.psum_scatter(
        after(moe_part, attn_grad), "tensor", scatter_dimension=0, tiled=True
    )
    block_out = (hidden_one + moe_local.astype(f32)).astype(bf16)

    output_mid_grad = nt(attn_grad, output_up).astype(bf16)
    attended_grad = (nt(attn_grad, output_full) + nn(output_mid_grad, output_down)).astype(bf16)
    grad_output_lower = tn(output_mid_grad, attended)
    output_mid_all = direct_sum(output_mid, "tensor", n_tensor).astype(bf16)
    grad_output_raise = tn(output_mid_all, columns_of(attn_grad))

    query_back, key_back, value_raw_grad, query_dot, key_dot = attend_back(
        (queries, keys, values), attended_grad, log_sums, raws, inverses, gains, tables
    )
    dots = direct_sum(jnp.stack([query_dot[:, 0], key_dot[:, 0]]), "tensor", n_tensor) / depth
    raw_grads = [
        (
            inverses[i] * (back - raws[i] * inverses[i] * dots[i][:, None])
        ).astype(bf16)
        for i, back in enumerate((query_back, key_back))
    ] + [value_raw_grad]
    mid_grads = [nt(raw_grads[i], raises[i]) for i in range(3)]
    mid_grads_wide = jnp.concatenate(mid_grads, axis=1)
    normed_part = nn(mid_grads_wide.astype(bf16), lowers)
    for i in range(3):
        normed_part = normed_part + nt(raw_grads[i], projections[:, i * width : (i + 1) * width])
    normed_grad = lax.psum_scatter(
        normed_part.astype(bf16), "tensor", scatter_dimension=0, tiled=True
    )
    input_grad = (
        hidden_grad + norm_back(rows_float, attn_gain_wide, normed_grad.astype(f32))
    ).astype(bf16)

    grad_raises = [tn(mids[:, i * rank : (i + 1) * rank], raw_grads[i]) for i in range(3)]
    mid_grads_all = direct_sum(mid_grads_wide, "tensor", n_tensor).astype(bf16)
    grad_lowers = tn(mid_grads_all, columns_of(normed))
    split = jnp.concatenate(grad_raises + [grad_output_lower], axis=0).astype(bf16)
    full = jnp.concatenate([grad_lowers, grad_output_raise], axis=0).astype(bf16)
    onehot = (adapter == jnp.arange(adapters, dtype=jnp.int32)).astype(f32)
    onehots = lax.all_gather(onehot, "dp", axis=0)
    split_all = lax.all_gather(split, "dp", axis=0)
    full_all = lax.all_gather(full, ("dp", "tensor"), axis=0)

    def by_adapter(pieces):
        return jnp.einsum("ga,grw->arw", onehots, pieces.astype(f32), precision="highest")

    split_sums = [
        by_adapter(split_all[:, i * rank : (i + 1) * rank]) for i in range(4)
    ]
    full_all = full_all.reshape(n_data, n_tensor, 4, rank, width)
    full_sums = [
        by_adapter(full_all[:, :, i].transpose(0, 2, 1, 3).reshape(n_data, rank, depth))
        for i in range(4)
    ]

    def turned(table):
        return table.transpose(0, 2, 1)

    return (
        block_out,
        input_grad,
        turned(full_sums[0]),
        split_sums[0],
        turned(full_sums[1]),
        split_sums[1],
        turned(full_sums[2]),
        split_sums[2],
        turned(split_sums[3]),
        full_sums[3],
    )


def solution(mesh):
    rows = P(("dp", "tensor"), None)
    raised = P(None, None, "tensor")
    in_specs = (
        rows,
        P(),
        P("tensor"),
        P("tensor"),
        P("dp", "tensor"),
        P("dp", "tensor"),
        P("dp", "tensor"),
        P("tensor", "dp"),
        P(),
        P("dp", None),
        P(None, "dp", "tensor"),
        P(None, "dp", "tensor"),
        P(None, "tensor", "dp"),
        P(),
        raised,
        P(),
        raised,
        P(),
        raised,
        P(None, "tensor", None),
        P(),
        P("dp", None),
        P("dp"),
        rows,
    )
    out_specs = (
        rows,
        rows,
        P(),
        raised,
        P(),
        raised,
        P(),
        raised,
        P(None, "tensor", None),
        P(),
    )
    return jax.shard_map(
        functools.partial(per_device, mesh.shape["dp"], mesh.shape["tensor"]),
        mesh=mesh,
        in_specs=in_specs,
        out_specs=out_specs,
        check_vma=False,
    )
```

```python
import functools

import jax
import jax.numpy as jnp
from jax import lax
from jax.experimental import pallas as pl
from jax.experimental.pallas import tpu as pltpu
from jax.sharding import PartitionSpec as P

HEAD_DIM = 128
EPSILON = 1e-05
ROPE_BASE = 10000.0
MASKED = -1e30
MIB = 1024 * 1024
CHUNKS = 2

f32 = jnp.float32
bf16 = jnp.bfloat16


def nn(left, right):
    return jnp.dot(left, right, preferred_element_type=f32)


def nt(left, right):
    return lax.dot_general(left, right, (((1,), (1,)), ((), ())), preferred_element_type=f32)


def tn(left, right):
    return lax.dot_general(left, right, (((0,), (0,)), ((), ())), preferred_element_type=f32)


def after(value, *others):
    return lax.optimization_barrier((value,) + others)[0]


def line_units(unit, axis, count):
    rights, lefts = [unit], [unit]
    for step in range(1, count):
        rights.append(
            lax.ppermute(rights[-1], axis, [(i, i + 1) for i in range(step - 1, count - 1)])
        )
        lefts.append(
            lax.ppermute(lefts[-1], axis, [(i, i - 1) for i in range(1, count - step + 1)])
        )
    return rights[1:], lefts[1:]


def direct_gather(value, axis, count):
    me = lax.axis_index(axis)
    whole = jnp.zeros((count,) + value.shape, value.dtype)
    whole = lax.dynamic_update_index_in_dim(whole, value, me, 0)
    for shift in range(1, count):
        got = lax.ppermute(value, axis, [(i, (i + shift) % count) for i in range(count)])
        whole = lax.dynamic_update_index_in_dim(whole, got, lax.rem(me - shift + count, count), 0)
    return whole


def data_exchanges(count):
    if count == 8:
        first = [i ^ (4 if i & 1 else 2) for i in range(count)]
        second = [i ^ (2 if i & 1 else 4) for i in range(count)]
        return [first, second, [i ^ 1 for i in range(count)]]
    bits = [1 << k for k in range(count.bit_length() - 1)]
    return [[i ^ bit for i in range(count)] for bit in reversed(bits)]


def direct_sum(value, axis, count):
    total = value
    for shift in range(1, count):
        total = total + lax.ppermute(
            value, axis, [(i, (i + shift) % count) for i in range(count)]
        )
    return total


def rope_tables(row_count):
    position = jnp.arange(row_count, dtype=jnp.int32).astype(f32)
    half = HEAD_DIM // 2
    frequency = ROPE_BASE ** (-2.0 * jnp.arange(half, dtype=f32) / HEAD_DIM)
    angles = position[:, None] * frequency[None, :]
    cosine, sine = jnp.cos(angles), jnp.sin(angles)
    return (
        jnp.concatenate([cosine, cosine], axis=1),
        jnp.concatenate([-sine, sine], axis=1),
    )


def as_row(wide):
    return jnp.sum(wide.T, axis=0, keepdims=True)


def as_columns(row):
    return jnp.broadcast_to(row, (128, row.shape[1])).T


def fold_lanes(values):
    total = values[:, :128]
    for first in range(128, values.shape[1], 128):
        total = total + values[:, first : first + 128]
    return total


def project_kernel(count, me, *refs):
    unit = refs[0]
    rights, lefts = refs[1:count], refs[count : 2 * count - 1]
    weights, lowers, query_up, key_up, value_up = refs[2 * count - 1 : 2 * count + 4]
    normed, query_raw, key_raw, values, mids, totals = refs[2 * count + 4 : 2 * count + 10]
    step = pl.program_id(0)
    width = query_up.shape[1]
    rank = query_up.shape[0]

    @pl.when(step == 0)
    def _():
        normed[...] = unit[...]

    for distance in range(1, count):

        @pl.when((step == distance) & (me[0] >= distance))
        def _():
            normed[...] = rights[distance - 1][...]

        @pl.when((step == distance) & (me[0] < distance))
        def _():
            normed[...] = lefts[count - distance - 1][...]

    rows = normed[...]
    mid = nt(rows, lowers[...]).astype(bf16)
    mids[...] = mid

    def raw(place, up):
        return nn(rows, weights[:, place * width : (place + 1) * width]) + nn(
            mid[:, place * rank : (place + 1) * rank], up[...]
        )

    query = raw(0, query_up)
    key = raw(1, key_up)
    query_raw[...] = query
    key_raw[...] = key
    values[...] = raw(2, value_up).astype(bf16)
    totals[0:1, :] = as_row(fold_lanes(query * query))
    totals[1:2, :] = as_row(fold_lanes(key * key))


def project(unit, rights, lefts, weights, lowers, ups, me):
    count = len(rights) + 1
    part, depth = unit.shape
    rows = part * count
    rank, width = ups[0].shape

    def fixed(shape):
        return pl.BlockSpec(shape, lambda s, p: (0, 0), pipeline_mode=pl.Buffered(1))

    def out(columns):
        return pl.BlockSpec((part, columns), lambda s, p: (lax.rem(p[0] - s + count, count), 0))

    return pl.pallas_call(
        functools.partial(project_kernel, count),
        grid_spec=pltpu.PrefetchScalarGridSpec(
            num_scalar_prefetch=1,
            grid=(count,),
            in_specs=[fixed((part, depth))] * (2 * count - 1)
            + [fixed(weights.shape), fixed(lowers.shape)]
            + [fixed((rank, width))] * 3,
            out_specs=[
                out(depth),
                out(width),
                out(width),
                out(width),
                out(3 * rank),
                pl.BlockSpec((2, part), lambda s, p: (0, lax.rem(p[0] - s + count, count))),
            ],
        ),
        out_shape=[
            jax.ShapeDtypeStruct((rows, depth), bf16),
            jax.ShapeDtypeStruct((rows, width), f32),
            jax.ShapeDtypeStruct((rows, width), f32),
            jax.ShapeDtypeStruct((rows, width), bf16),
            jax.ShapeDtypeStruct((rows, 3 * rank), bf16),
            jax.ShapeDtypeStruct((2, rows), f32),
        ],
        compiler_params=pltpu.CompilerParams(vmem_limit_bytes=50 * MIB),
        cost_estimate=pl.CostEstimate(
            flops=6 * rows * depth * width, bytes_accessed=24 * MIB, transcendentals=0
        ),
    )(me[None], unit, *rights, *lefts, weights, lowers, *ups)


def causal_scores(q_block, keys, first):
    scores = nt(q_block, keys) * (HEAD_DIM**-0.5)
    rows = first + lax.broadcasted_iota(jnp.int32, scores.shape, 0)
    columns = lax.broadcasted_iota(jnp.int32, scores.shape, 1)
    return jnp.where(columns <= rows, scores, MASKED)


def attend_kernel(
    block,
    query_raw,
    key_raw,
    values,
    inverses,
    query_gain,
    key_gain,
    cosine,
    sine,
    queries,
    keys,
    attended,
    log_sums,
    wide_inverses,
):
    half = HEAD_DIM // 2
    rows = query_raw.shape[0]

    @pl.when(pl.program_id(0) == 0)
    def _():
        wide_inverses[0] = as_columns(inverses[0:1, :])
        wide_inverses[1] = as_columns(inverses[1:2, :])

    def rotated(raw, place, gain):
        head = raw[...] * wide_inverses[place] * gain[...]
        return (head * cosine[...] + pltpu.roll(head, half, 1) * sine[...]).astype(bf16)

    queries[...] = rotated(query_raw, 0, query_gain)
    keys[...] = rotated(key_raw, 1, key_gain)
    for first in range(0, rows, block):
        end = first + block
        here = slice(first, end)
        scores = causal_scores(queries[here, :], keys[0:end, :], first)
        top = jnp.max(scores, axis=1, keepdims=True)
        exponent = jnp.exp(scores - top)
        total = jnp.sum(exponent, axis=1, keepdims=True)
        soft = (exponent * (1.0 / total)).astype(bf16)
        attended[here, :] = nn(soft, values[0:end, :]).astype(bf16)
        log_sums[0, here, :] = top + jnp.log(total)


def attend(raws, values, inverses, gains, tables):
    rows, width = values.shape
    heads = width // HEAD_DIM
    by_head = pl.BlockSpec((rows, HEAD_DIM), lambda h: (0, h))
    stats = pl.BlockSpec((2, rows), lambda h: (0, 0))
    gain = pl.BlockSpec((1, HEAD_DIM), lambda h: (0, h))
    table = pl.BlockSpec((rows, HEAD_DIM), lambda h: (0, 0))
    wide = jax.ShapeDtypeStruct((rows, width), bf16)
    return pl.pallas_call(
        functools.partial(attend_kernel, min(256, rows)),
        grid=(heads,),
        in_specs=[by_head] * 3 + [stats] + [gain] * 2 + [table] * 2,
        out_specs=[by_head] * 3 + [pl.BlockSpec((1, rows, 1), lambda h: (h, 0, 0))],
        out_shape=[wide] * 3 + [jax.ShapeDtypeStruct((heads, rows, 1), f32)],
        scratch_shapes=[pltpu.VMEM((2, rows, 128), f32)],
        compiler_params=pltpu.CompilerParams(vmem_limit_bytes=40 * MIB),
        cost_estimate=pl.CostEstimate(
            flops=2 * rows * rows * width,
            bytes_accessed=20 * rows * width,
            transcendentals=rows * rows * heads // 2,
        ),
    )(*raws, values, inverses, *gains, *tables)


def attend_back_kernel(
    block,
    queries,
    keys,
    values,
    grads,
    log_sums,
    query_raw,
    key_raw,
    inverses,
    query_gain,
    key_gain,
    cosine,
    sine,
    query_out,
    key_out,
    value_out,
    dots,
    query_grad,
    key_grad,
    value_grad,
    wide_inverses,
    dot_sums,
):
    half = HEAD_DIM // 2
    rows = queries.shape[0]
    scale = HEAD_DIM**-0.5

    @pl.when(pl.program_id(0) == 0)
    def _():
        wide_inverses[0] = as_columns(inverses[0:1, :])
        wide_inverses[1] = as_columns(inverses[1:2, :])
        dot_sums[...] = jnp.zeros_like(dot_sums)

    for first in range(rows - block, -1, -block):
        end = first + block
        here = slice(first, end)
        scores = causal_scores(queries[here, :], keys[0:end, :], first)
        soft = jnp.exp(scores - log_sums[0, here, :])
        soft_grad = nt(grads[here, :], values[0:end, :])
        inner = jnp.sum(soft * soft_grad, axis=1, keepdims=True)
        score_grad = (soft * (soft_grad - inner)).astype(bf16)
        value_part = tn(soft.astype(bf16), grads[here, :])
        key_part = tn(score_grad, queries[here, :])
        query_grad[here, :] = nn(score_grad, keys[0:end, :])
        if end == rows:
            value_grad[...] = value_part
            key_grad[...] = key_part
        else:
            value_grad[0:end, :] += value_part
            key_grad[0:end, :] += key_part

    def pulled(grad, raw, place, gain, out):
        turned = grad[...] * scale
        turned = turned * cosine[...] - pltpu.roll(turned, half, 1) * sine[...]
        turned = turned * gain[...]
        out[...] = turned
        dot_sums[place] += turned * (raw[...] * wide_inverses[place])

    pulled(query_grad, query_raw, 0, query_gain, query_out)
    pulled(key_grad, key_raw, 1, key_gain, key_out)
    value_out[...] = value_grad[...].astype(bf16)

    @pl.when(pl.program_id(0) == pl.num_programs(0) - 1)
    def _():
        dots[0:1, :] = as_row(dot_sums[0])
        dots[1:2, :] = as_row(dot_sums[1])


def attend_back(heads_in, grads, log_sums, raws, inverses, gains, tables):
    rows, width = grads.shape
    heads = width // HEAD_DIM
    by_head = pl.BlockSpec((rows, HEAD_DIM), lambda h: (0, h))
    stats = pl.BlockSpec((2, rows), lambda h: (0, 0))
    gain = pl.BlockSpec((1, HEAD_DIM), lambda h: (0, h))
    table = pl.BlockSpec((rows, HEAD_DIM), lambda h: (0, 0))
    return pl.pallas_call(
        functools.partial(attend_back_kernel, min(256, rows)),
        grid=(heads,),
        in_specs=[by_head] * 4
        + [pl.BlockSpec((1, rows, 1), lambda h: (h, 0, 0))]
        + [by_head] * 2
        + [stats]
        + [gain] * 2
        + [table] * 2,
        out_specs=[by_head] * 3 + [stats],
        out_shape=[
            jax.ShapeDtypeStruct((rows, width), f32),
            jax.ShapeDtypeStruct((rows, width), f32),
            jax.ShapeDtypeStruct((rows, width), bf16),
            jax.ShapeDtypeStruct((2, rows), f32),
        ],
        scratch_shapes=[pltpu.VMEM((rows, HEAD_DIM), f32)] * 3
        + [pltpu.VMEM((2, rows, 128), f32)] * 2,
        compiler_params=pltpu.CompilerParams(vmem_limit_bytes=50 * MIB),
        cost_estimate=pl.CostEstimate(
            flops=5 * rows * rows * width,
            bytes_accessed=28 * rows * width,
            transcendentals=rows * rows * heads // 2,
        ),
    )(*heads_in, grads, log_sums, *raws, inverses, *gains, *tables)


def project_back_kernel(
    query_back,
    key_back,
    value_grads,
    query_raw,
    key_raw,
    inverses,
    dots,
    weights,
    lowers,
    query_up,
    key_up,
    value_up,
    part,
    raw_grads,
    mid_grads,
):
    width = query_back.shape[1]
    rank = query_up.shape[0]

    def raw_grad(back, raw, place):
        inverse = as_columns(inverses[place : place + 1, :])
        dot = as_columns(dots[place : place + 1, :]) * inverse
        for first in range(0, width, 128):
            here = slice(first, first + 128)
            grad = inverse * (back[:, here] - raw[:, here] * dot)
            raw_grads[:, place * width + first : place * width + first + 128] = grad.astype(bf16)

    raw_grad(query_back, query_raw, 0)
    raw_grad(key_back, key_raw, 1)
    raw_grads[:, 2 * width :] = value_grads[...]
    total = nt(raw_grads[...], weights[...])
    for place, up in enumerate((query_up, key_up, value_up)):
        here = slice(place * rank, (place + 1) * rank)
        mid = nt(raw_grads[:, place * width : (place + 1) * width], up[...])
        mid_grads[:, here] = mid
        total += nn(mid.astype(bf16), lowers[here, :])
    part[...] = total.astype(bf16)


def project_back(backs, value_grads, raws, inverses, dots, weights, lowers, ups):
    rows, width = value_grads.shape
    rank = ups[0].shape[0]
    depth = weights.shape[0]
    block = min(256, rows)

    def fixed(shape):
        return pl.BlockSpec(shape, lambda s: (0, 0), pipeline_mode=pl.Buffered(1))

    def rowwise(columns):
        return pl.BlockSpec((block, columns), lambda s: (s, 0))

    stats = pl.BlockSpec((2, block), lambda s: (0, s))
    return pl.pallas_call(
        project_back_kernel,
        grid=(rows // block,),
        in_specs=[rowwise(width)] * 5
        + [stats] * 2
        + [fixed(weights.shape), fixed(lowers.shape)]
        + [fixed((rank, width))] * 3,
        out_specs=[rowwise(depth), rowwise(3 * width), rowwise(3 * rank)],
        out_shape=[
            jax.ShapeDtypeStruct((rows, depth), bf16),
            jax.ShapeDtypeStruct((rows, 3 * width), bf16),
            jax.ShapeDtypeStruct((rows, 3 * rank), f32),
        ],
        compiler_params=pltpu.CompilerParams(vmem_limit_bytes=50 * MIB),
        cost_estimate=pl.CostEstimate(
            flops=6 * rows * depth * width, bytes_accessed=24 * MIB, transcendentals=0
        ),
    )(*backs, value_grads, *raws, inverses, dots, weights, lowers, *ups)


def experts_kernel(pieces, group, splits, sources, rows_in, grads, weight, *refs):
    shards = refs[:pieces]
    moe, back, gates, ups, downs, moe_sum, back_sum, slots, arrived = refs[-9:]
    step = pl.program_id(0)
    steps = pl.num_programs(0)
    rows, experts = weight.shape
    depth = moe_sum.shape[1]
    wide = depth // pieces
    hidden = gates.shape[-1]

    def copies(at_step, slot):
        made = []
        for index in range(pieces):
            place = pl.ds(pl.multiple_of(sources[index] * wide, wide), wide)
            for member in range(group):
                expert = at_step * group + member
                targets = (
                    gates.at[slot, member, place],
                    ups.at[slot, member, place],
                    downs.at[slot, pl.ds(member * hidden, hidden), place],
                )
                for kind, target in enumerate(targets):
                    made.append(
                        pltpu.make_async_copy(
                            shards[index].at[kind * experts + expert],
                            target,
                            arrived.at[slot, kind, member, index],
                        )
                    )
        return made

    @pl.when(step == 0)
    def _():
        for copy in copies(0, 0):
            copy.start()
        slots[...] = jnp.zeros_like(slots)
        moe_sum[...] = jnp.zeros_like(moe_sum)
        back_sum[...] = jnp.zeros_like(back_sum)

    slot = lax.rem(step, 2)

    @pl.when(step + 1 < steps)
    def _():
        for copy in copies(step + 1, 1 - slot):
            copy.start()

    for copy in copies(step, slot):
        copy.wait()

    grads_all = grads[...].reshape(rows, depth)
    down = downs[slot]
    part = rows // splits
    for split in range(splits):
        here = slice(split * part, (split + 1) * part)
        row_block = rows_in[here, :]
        weight_block = weight[here, :]
        lane = lax.broadcasted_iota(jnp.int32, weight_block.shape, 1)
        inner_all = nt(grads_all[here, :], down)
        scaled_all = []
        back_block = None
        slot_block = None
        for member in range(group):
            expert = step * group + member
            gate = nn(row_block, gates[slot, member])
            up = nn(row_block, ups[slot, member])
            inner = inner_all[:, member * hidden : (member + 1) * hidden]
            row_scale = jnp.sum(
                jnp.where(lane == expert, weight_block, 0.0), axis=1, keepdims=True
            )
            sigmoid = jax.nn.sigmoid(gate)
            silu = gate * sigmoid
            activated = (silu * up).astype(bf16).astype(f32)
            slot_grad = jnp.where(
                lane == expert, jnp.sum(activated * inner, axis=1, keepdims=True), 0.0
            )
            scaled_all.append((row_scale * activated).astype(bf16))
            inner = row_scale * inner
            gate_grad = (inner * up * (sigmoid * (1.0 + gate * (1.0 - sigmoid)))).astype(bf16)
            up_grad = (inner * silu).astype(bf16)
            back_part = nt(gate_grad, gates[slot, member]) + nt(up_grad, ups[slot, member])
            back_block = back_part if back_block is None else back_block + back_part
            slot_block = slot_grad if slot_block is None else slot_block + slot_grad
        scaled = scaled_all[0] if group == 1 else jnp.concatenate(scaled_all, axis=1)
        slots[here, :] += slot_block
        moe_sum[here, :] += nn(scaled, down)
        back_sum[here, :] += back_block

    @pl.when(step == steps - 1)
    def _():
        moe[...] = moe_sum[...].astype(bf16).reshape(moe.shape)
        back[:, :depth] = back_sum[...].astype(bf16)
        back[:, depth:] = jnp.zeros((rows, back.shape[1] - depth), bf16)
        back[:, depth : depth + experts] = slots[...].astype(bf16)


def experts_both(rows_in, grads, weight, shards, sources, chunk, earlier):
    rows, depth = rows_in.shape
    units, _, part, _ = grads.shape
    experts = weight.shape[1]
    pieces = len(shards)
    hidden = shards[0].shape[2]
    group = 2

    def fixed(shape):
        return pl.BlockSpec(shape, lambda e, s: (0, 0), pipeline_mode=pl.Buffered(1))

    of_chunk = pl.BlockSpec(
        (units, 1, part, depth), lambda e, s: (0, chunk, 0, 0), pipeline_mode=pl.Buffered(1)
    )
    anywhere = pl.BlockSpec(memory_space=pl.ANY)
    in_specs = [fixed((rows, depth)), of_chunk, fixed((rows, experts))] + [anywhere] * pieces
    operands = [rows_in, grads, weight, *shards]
    aliases = {}
    if earlier is not None:
        in_specs.append(anywhere)
        operands.append(earlier)
        aliases = {len(operands): 0}
    return pl.pallas_call(
        functools.partial(experts_kernel, pieces, group, 2),
        grid_spec=pltpu.PrefetchScalarGridSpec(
            num_scalar_prefetch=1,
            grid=(experts // group,),
            in_specs=in_specs,
            out_specs=[of_chunk, fixed((rows, depth + 128))],
            scratch_shapes=[
                pltpu.VMEM((2, group, depth, hidden), bf16),
                pltpu.VMEM((2, group, depth, hidden), bf16),
                pltpu.VMEM((2, group * hidden, depth), bf16),
                pltpu.VMEM((rows, depth), f32),
                pltpu.VMEM((rows, depth), f32),
                pltpu.VMEM((rows, experts), f32),
                pltpu.SemaphoreType.DMA((2, 3, group, pieces)),
            ],
        ),
        out_shape=[
            jax.ShapeDtypeStruct(grads.shape, bf16),
            jax.ShapeDtypeStruct((rows, depth + 128), bf16),
        ],
        input_output_aliases=aliases,
        compiler_params=pltpu.CompilerParams(vmem_limit_bytes=58 * MIB),
        cost_estimate=pl.CostEstimate(
            flops=12 * rows * depth * hidden * experts,
            bytes_accessed=6 * depth * hidden * experts,
            transcendentals=rows * hidden * experts,
        ),
    )(sources, *operands)


def norm_back(values, gain, grad):
    inverse = lax.rsqrt(jnp.mean(values * values, axis=-1, keepdims=True) + EPSILON)
    scaled = values * inverse
    inner = gain * grad
    return inverse * (inner - scaled * jnp.mean(inner * scaled, axis=-1, keepdims=True))


def norm_rows(values, gain):
    inverse = lax.rsqrt(jnp.mean(values * values, axis=-1, keepdims=True) + EPSILON)
    return values * inverse * gain


def per_device(
    n_data,
    n_tensor,
    tokens,
    attn_gain,
    query_gain,
    key_gain,
    query_weight,
    key_weight,
    value_weight,
    output_weight,
    mlp_gain,
    router_weight,
    gate_weight,
    up_weight,
    down_weight,
    query_lower,
    query_raise,
    key_lower,
    key_raise,
    value_lower,
    value_raise,
    output_lower,
    output_raise,
    routes,
    adapter_choice_rows,
    out_cotangent,
):
    local_rows, depth = tokens.shape
    rows = local_rows * n_tensor
    width = query_weight.shape[1]
    adapters, rank = query_raise.shape[:2]
    experts = router_weight.shape[1]
    me = lax.axis_index("tensor")
    first_row = me * local_rows
    adapter = adapter_choice_rows[0]

    def chosen(table):
        return lax.dynamic_index_in_dim(table, adapter, 0, keepdims=False)

    def columns_of(matrix):
        return lax.dynamic_slice_in_dim(matrix, me * width, width, 1)

    attn_gain_wide = attn_gain.astype(f32)
    mlp_gain_wide = mlp_gain.astype(f32)
    gains = (query_gain.astype(f32)[None, :], key_gain.astype(f32)[None, :])
    expert_ids = jnp.arange(experts, dtype=jnp.int32)

    projections = lax.all_gather(
        jnp.concatenate([query_weight, key_weight, value_weight], axis=1),
        "dp",
        axis=0,
        tiled=True,
    )
    output_and_router = lax.all_gather(
        jnp.concatenate([output_weight, router_weight.T], axis=0), "dp", axis=0
    )
    output_full = output_and_router[:, :width].transpose(1, 0, 2).reshape(width, depth)
    router_full = output_and_router[:, width:].transpose(1, 0, 2).reshape(experts, depth)

    rows_float = tokens.astype(f32)
    normed_local = norm_rows(rows_float, attn_gain_wide).astype(bf16)

    exchanges = data_exchanges(n_data)

    def swap(value, partners):
        return lax.ppermute(value, "dp", list(enumerate(partners)))

    sources = [list(range(n_data))]
    for partners in exchanges:
        sources += [[known[partner] for partner in partners] for known in sources]
    my_sources = jnp.array(sources, jnp.int32).T[lax.axis_index("dp")]
    shard = jnp.concatenate(
        [after(gate_weight, normed_local), up_weight, down_weight], axis=0
    )
    shards = [shard]

    rights, lefts = line_units(normed_local, "tensor", n_tensor)
    cotangent_full = lax.all_gather(out_cotangent, "tensor", axis=0, tiled=True)
    tables = rope_tables(rows)
    lowers = jnp.concatenate(
        [chosen(query_lower).T, chosen(key_lower).T, chosen(value_lower).T], axis=0
    )
    raises = [chosen(query_raise), chosen(key_raise), chosen(value_raise)]
    normed, query_raw, key_raw, values, mids, totals = project(
        normed_local, rights, lefts, projections, lowers, raises, me
    )
    raws = (query_raw, key_raw)
    inverses = lax.rsqrt(direct_sum(totals, "tensor", n_tensor) / depth + EPSILON)
    queries, keys, attended, log_sums = attend(raws, values, inverses, gains, tables)

    for number, partners in enumerate(exchanges):
        held = []
        for index, piece in enumerate(shards):
            if index == 0:
                held.append(swap(piece, partners))
            elif number < len(exchanges) - 1 or index < len(shards) - 1:
                held.append(swap(after(piece, attended), partners))
            else:
                held.append(None)
        shards += held

    output_down = chosen(output_lower).T
    output_up = chosen(output_raise)
    output_mid = nt(attended, output_down)
    attn_part = nn(attended, output_full) + nn(output_mid.astype(bf16), output_up)
    hidden_one = rows_float + lax.psum_scatter(
        attn_part.astype(bf16), "tensor", scatter_dimension=0, tiled=True
    ).astype(f32)
    normed_two = norm_rows(hidden_one, mlp_gain_wide).astype(bf16)
    last = len(shards) // 2 - 1
    shards[-1] = swap(after(shards[last], normed_two), exchanges[-1])

    prob_local = jax.nn.softmax(nt(normed_two, router_full), axis=-1)
    part = local_rows // CHUNKS
    grads_view = cotangent_full.reshape(n_tensor, CHUNKS, part, depth)
    routes_view = routes.reshape(n_tensor, CHUNKS, part, routes.shape[1])
    moe_part = None
    back_parts = []
    for chunk in range(CHUNKS):
        chunk_rows = lax.all_gather(
            normed_two[chunk * part : (chunk + 1) * part], "tensor", axis=0, tiled=True
        )
        chunk_routes = routes_view[:, chunk].reshape(n_tensor * part, routes.shape[1])
        chosen_experts = jnp.any(chunk_routes[:, :, None] == expert_ids[None, None, :], axis=1)
        probability = jax.nn.softmax(nt(chunk_rows, router_full), axis=-1)
        moe_part, back_part = experts_both(
            chunk_rows,
            grads_view,
            jnp.where(chosen_experts, probability, 0.0),
            shards,
            my_sources,
            chunk,
            moe_part,
        )
        back_parts.append(
            lax.psum_scatter(back_part, "tensor", scatter_dimension=0, tiled=True)
        )
    back_local = jnp.concatenate(back_parts, axis=0).astype(f32)
    local_routes = lax.dynamic_slice_in_dim(routes, first_row, local_rows, 0)
    local_mask = jnp.any(local_routes[:, :, None] == expert_ids[None, None, :], axis=1)
    prob_grad = jnp.where(local_mask, back_local[:, depth : depth + experts], 0.0)
    logit_grad = (
        prob_local * (prob_grad - jnp.sum(prob_local * prob_grad, axis=1, keepdims=True))
    ).astype(bf16)
    normed_two_grad = back_local[:, :depth] + nn(logit_grad, router_full)
    hidden_grad = out_cotangent.astype(f32) + norm_back(
        hidden_one, mlp_gain_wide, normed_two_grad
    )
    attn_grad = lax.all_gather(hidden_grad.astype(bf16), "tensor", axis=0, tiled=True)
    moe_local = lax.psum_scatter(
        after(moe_part.reshape(rows, depth), attn_grad), "tensor", scatter_dimension=0, tiled=True
    )
    block_out = (hidden_one + moe_local.astype(f32)).astype(bf16)

    output_mid_grad = nt(attn_grad, output_up).astype(bf16)
    attended_grad = (nt(attn_grad, output_full) + nn(output_mid_grad, output_down)).astype(bf16)
    query_back, key_back, value_grads, dots = attend_back(
        (queries, keys, values), attended_grad, log_sums, raws, inverses, gains, tables
    )
    dots = direct_sum(dots, "tensor", n_tensor) / depth
    normed_part, raw_grads, mid_grads = project_back(
        (query_back, key_back), value_grads, raws, inverses, dots, projections, lowers, raises
    )
    normed_grad = lax.psum_scatter(normed_part, "tensor", scatter_dimension=0, tiled=True)
    input_grad = (
        hidden_grad + norm_back(rows_float, attn_gain_wide, normed_grad.astype(f32))
    ).astype(bf16)

    grad_output_lower = tn(output_mid_grad, attended)
    sums = direct_sum(jnp.concatenate([mid_grads, output_mid], axis=1), "tensor", n_tensor)
    grad_lowers = tn(sums[:, : 3 * rank].astype(bf16), columns_of(normed))
    grad_output_raise = tn(sums[:, 3 * rank :].astype(bf16), columns_of(attn_grad))
    grad_raises = tn(mids, raw_grads)
    grad_raises = [
        grad_raises[i * rank : (i + 1) * rank, i * width : (i + 1) * width] for i in range(3)
    ]
    full = jnp.concatenate([grad_lowers, grad_output_raise], axis=0).astype(bf16)
    full = direct_gather(full, "tensor", n_tensor).reshape(n_tensor * 4 * rank, width)
    onehot = jnp.broadcast_to(
        (adapter == jnp.arange(adapters, dtype=jnp.int32)).astype(bf16)[:, None],
        (adapters, width),
    )
    onehot = jnp.concatenate([onehot, jnp.zeros((16 - adapters, width), bf16)], axis=0)
    split = jnp.concatenate(grad_raises + [grad_output_lower], axis=0).astype(bf16)
    gathered = jnp.concatenate([full, split, onehot], axis=0)[None]
    for partners in reversed(data_exchanges(n_data)[:-1]):
        gathered = jnp.concatenate([gathered, swap(gathered, partners)], axis=0)
    gathered = jnp.concatenate([gathered, swap(gathered, exchanges[-1])], axis=0)
    onehots = gathered[:, -16 : adapters - 16, 0]
    by_adapter = jnp.einsum(
        "ga,grw->arw", onehots, gathered[:, :-16], preferred_element_type=f32
    )
    split_sums = [
        by_adapter[:, (4 * n_tensor + i) * rank : (4 * n_tensor + i + 1) * rank]
        for i in range(4)
    ]
    full_sums = by_adapter[:, : 4 * n_tensor * rank].reshape(
        adapters, n_tensor, 4, rank, width
    )
    full_sums = [
        full_sums[:, :, i].transpose(0, 2, 1, 3).reshape(adapters, rank, depth) for i in range(4)
    ]

    def turned(table):
        return table.transpose(0, 2, 1)

    return (
        block_out,
        input_grad,
        turned(full_sums[0]),
        split_sums[0],
        turned(full_sums[1]),
        split_sums[1],
        turned(full_sums[2]),
        split_sums[2],
        turned(split_sums[3]),
        full_sums[3],
    )


def solution(mesh):
    rows = P(("dp", "tensor"), None)
    raised = P(None, None, "tensor")
    in_specs = (
        rows,
        P(),
        P("tensor"),
        P("tensor"),
        P("dp", "tensor"),
        P("dp", "tensor"),
        P("dp", "tensor"),
        P("tensor", "dp"),
        P(),
        P("dp", None),
        P(None, "dp", "tensor"),
        P(None, "dp", "tensor"),
        P(None, "tensor", "dp"),
        P(),
        raised,
        P(),
        raised,
        P(),
        raised,
        P(None, "tensor", None),
        P(),
        P("dp", None),
        P("dp"),
        rows,
    )
    out_specs = (
        rows,
        rows,
        P(),
        raised,
        P(),
        raised,
        P(),
        raised,
        P(None, "tensor", None),
        P(),
    )
    return jax.shard_map(
        functools.partial(per_device, mesh.shape["dp"], mesh.shape["tensor"]),
        mesh=mesh,
        in_specs=in_specs,
        out_specs=out_specs,
        check_vma=False,
    )
```
